128 devices in a mesh: group: 4 (over z), expert: 32 (over x, y, core).
Axes of the slice: x: 4, y: 4, z: 4, core: 2. Of those that a mesh axis runs over, the one named last changes fastest.
Arguments:
- quant_rows: bfloat16 [2, 4096, 3584], P(None, ('group', 'expert')), may hold values from -6 to 6
- row_scales: float32 [2, 4096, 28], P(None, ('group', 'expert')), may hold values from 0.25 to 4
- expert_ids: int32 [2, 4096, 8], P(None, ('group', 'expert')), may hold values from 0 to 127, as said below
- gate_weights: float32 [2, 4096, 8], P(None, ('group', 'expert')), may hold values from 0.1 to 1
- w_gate: bfloat16 [128, 3584, 1024], P(('group', 'expert')), may hold values from -0.09375 to 0.09375
- w_up: bfloat16 [128, 3584, 1024], P(('group', 'expert')), may hold values from -0.09375 to 0.09375
- w_down: bfloat16 [128, 1024, 3584], P(('group', 'expert')), may hold values from -0.1875 to 0.1875
Outputs:
- mixed: bfloat16 [2, 4096, 3584], P(None, ('group', 'expert'))
The draws below stay inside these ranges and needn't reach their ends.
Inputs may be any that keep to these rules, and one draw needn't show every extreme that they name: `expert_ids`: each token names 8 different experts, 4 in each of exactly 2 groups (expert e lies in group e // 32). In an aligned block of 32 rows of one micro-batch (the rows of one device), one group is common to all tokens, every expert of that group is named by exactly 4 tokens, and no expert is named by more than 4.
All inputs are finite; a program needn't handle non-finite values.
Results may differ from the reference program's by a relative error of at most 0.025.
Values may be sent and summed in bfloat16 or wider, within the bound.
No kernel may reach another device: no remote copies, remote signals or barrier semaphores. Data moves between devices by JAX's collectives and lax.ppermute only.
A program may use at most 128 MiB of HBM per device.

```python
import math
import jax
import jax.numpy as jnp
from jax import lax

D = 3584
FF = 1024
TOPK = 8
GROUPS_LIM = 2
BLOCK = 128
MB = 2
CAP = 4
EXPERTS = 128
TOK_DEV = 32
TOKENS = 4096
N_GROUP = 4
N_EXPERT = 32


def draw_expert_ids(key, part):
    key = jax.random.fold_in(key, 7)
    n_blocks = MB * EXPERTS
    per_group = TOPK // GROUPS_LIM
    keys = jax.random.split(key, 5)
    home_group = jax.random.randint(keys[0], (n_blocks,), 0, N_GROUP).astype(jnp.int32)
    second_group = ((home_group[:, None] + jax.random.randint(keys[1], (n_blocks, TOK_DEV), 1, N_GROUP)) % N_GROUP).astype(jnp.int32)
    order_keys = jax.random.split(keys[2], n_blocks * N_GROUP)
    orders = jax.vmap(lambda sub: jax.random.permutation(sub, N_EXPERT))(order_keys).reshape(n_blocks, N_GROUP, N_EXPERT).astype(jnp.int32)
    offsets = jax.random.randint(keys[3], (n_blocks, N_GROUP), 0, N_EXPERT).astype(jnp.int32)
    block_index = jnp.arange(n_blocks, dtype=jnp.int32)
    token_index = jnp.arange(TOK_DEV, dtype=jnp.int32)
    within = jnp.arange(per_group, dtype=jnp.int32)
    home_offset = offsets[block_index, home_group]
    home_pos = (home_offset[:, None, None] + per_group * token_index[None, :, None] + within[None, None, :]) % N_EXPERT
    home_order = orders[block_index, home_group]
    home_inner = jnp.take_along_axis(home_order, home_pos.reshape(n_blocks, -1), axis=1).reshape(n_blocks, TOK_DEV, per_group)
    onehot = (second_group[:, :, None] == jnp.arange(N_GROUP, dtype=jnp.int32)[None, None, :]).astype(jnp.int32)
    earlier = jnp.sum((jnp.cumsum(onehot, axis=1) - onehot) * onehot, axis=2)
    second_offset = jnp.take_along_axis(offsets, second_group, axis=1)
    second_pos = (second_offset[:, :, None] + per_group * earlier[:, :, None] + within[None, None, :]) % N_EXPERT
    second_order = orders[block_index[:, None], second_group]
    second_inner = jnp.take_along_axis(second_order, second_pos, axis=2)
    chosen = jnp.concatenate([home_group[:, None, None] * N_EXPERT + home_inner, second_group[:, :, None] * N_EXPERT + second_inner], axis=2)
    chosen = jax.random.permutation(keys[4], chosen, axis=2, independent=True)
    return chosen.reshape(MB, TOKENS, TOPK).astype(jnp.int32)


def block_scale(stream_key, dims, pieces, low, high):
    gain, own = 1.0, jax.random.fold_in(stream_key, 6)
    for position, blocks in pieces:
        draws = jnp.exp(jax.random.uniform(jax.random.fold_in(own, position), (blocks,), jnp.float32, low / len(pieces), high / len(pieces)))
        gain = gain * jnp.repeat(draws, dims[position] // blocks).reshape([-1 if axis == position else 1 for axis in range(len(dims))])
    return gain


def scatter_about(own_key, shape, spread, bound, shards=(), held_as=jnp.bfloat16):
    result = spread * jax.random.normal(own_key, shape, jnp.float32)
    if shards:
        result = result * block_scale(own_key, shape, shards, -0.22, 0.18)
    return jnp.clip(result, -bound, bound).astype(held_as)


def setup_inputs(seed: int = 0) -> dict:
    seeds = jax.random.split(jax.random.key(seed), 8)
    return {
        "quant_rows": scatter_about(seeds[0], (MB, TOKENS, D), 1.0, 6.0, ((1, 128),)),
        "row_scales": jnp.clip(jnp.exp(math.log(4.0) - 2.7725887 * jax.random.uniform(seeds[1], (MB, TOKENS, D // BLOCK), jnp.float32) ** block_scale(seeds[1], (MB, TOKENS, D // BLOCK), ((1, 128),), -0.2, 0.2)), 0.25, 4.0),
        "expert_ids": draw_expert_ids(jax.random.fold_in(seeds[7], 71), 0),
        "gate_weights": jnp.clip(jnp.exp(math.log(1.0) - 2.3025851 * jax.random.uniform(seeds[3], (MB, TOKENS, TOPK), jnp.float32) ** block_scale(seeds[3], (MB, TOKENS, TOPK), ((1, 128),), -0.2, 0.2)), 0.1, 1.0),
        "w_gate": scatter_about(seeds[4], (EXPERTS, D, FF), D ** -0.5, 0.09375, ((0, 128),)),
        "w_up": scatter_about(seeds[5], (EXPERTS, D, FF), D ** -0.5, 0.09375, ((0, 128),)),
        "w_down": scatter_about(seeds[6], (EXPERTS, FF, D), FF ** -0.5, 0.1875, ((0, 128),)),
    }


def dequantize(quant, scales):
    rows = quant.shape[0]
    values = quant.astype(jnp.float32).reshape(rows, D // BLOCK, BLOCK) * scales[:, :, None]
    return values.reshape(rows, D).astype(jnp.bfloat16)


def expert_apply(rows, gate_w, up_w, down_w):
    gate = jnp.dot(rows, gate_w, preferred_element_type=jnp.float32)
    upper = jnp.dot(rows, up_w, preferred_element_type=jnp.float32)
    hidden = (jax.nn.silu(gate) * upper).astype(jnp.bfloat16)
    return jnp.dot(hidden, down_w, preferred_element_type=jnp.float32).astype(jnp.bfloat16)


def one_batch(quant, scales, ids, gates, w_gate, w_up, w_down):
    tokens_x = dequantize(quant, scales)
    blocks = ids.reshape(EXPERTS, TOK_DEV * TOPK)
    onehot = (blocks[:, :, None] == jnp.arange(EXPERTS, dtype=jnp.int32)[None, None, :]).astype(jnp.int32)
    before = jnp.cumsum(onehot, axis=1) - onehot
    rank = jnp.sum(before * onehot, axis=2)
    source = jnp.arange(EXPERTS, dtype=jnp.int32)[:, None]
    slot = (blocks * (EXPERTS * CAP) + source * CAP + rank).reshape(-1).astype(jnp.int32)
    token = (jnp.arange(TOKENS * TOPK, dtype=jnp.int32) // TOPK).astype(jnp.int32)
    table = jnp.zeros((EXPERTS * EXPERTS * CAP,), jnp.int32).at[slot].set(token + 1)
    table = table.reshape(EXPERTS, EXPERTS * CAP)

    def serve(items):
        index, gate_w, up_w, down_w = items
        live = index > 0
        picked = tokens_x[jnp.maximum(index - 1, 0)]
        rows = jnp.where(live[:, None], picked, jnp.zeros_like(picked))
        return expert_apply(rows, gate_w, up_w, down_w)

    outputs = lax.map(serve, (table, w_gate, w_up, w_down))
    outputs = outputs.reshape(EXPERTS * EXPERTS * CAP, D)
    chosen = outputs[slot].reshape(TOKENS, TOPK, D).astype(jnp.float32)
    total = jnp.sum(gates[:, :, None] * chosen, axis=1)
    return total.astype(jnp.bfloat16)


def reference(quant_rows, row_scales, expert_ids, gate_weights, w_gate, w_up, w_down):
    results = []
    for batch in range(MB):
        results.append(one_batch(quant_rows[batch], row_scales[batch], expert_ids[batch], gate_weights[batch], w_gate, w_up, w_down))
    return jnp.stack(results, axis=0)
```

```python
import functools

import jax
import jax.numpy as jnp
from jax import lax
from jax.experimental import pallas as pl
from jax.experimental.pallas import tpu as pltpu
from jax.sharding import PartitionSpec as P

BLOCK = 128
CAP = 4
VMEM_LIMIT = 60 * 1024 * 1024


def place_kernel(quant_ref, scale_ref, ids_ref, gate_ref, send_ref, weight_ref, slot_ref):
    tokens = quant_ref.shape[0] * quant_ref.shape[1]
    slots = slot_ref.shape[0]
    batches, topk, rows = ids_ref.shape

    @pl.when(pl.program_id(0) == 0)
    def _():
        row = lax.broadcasted_iota(jnp.int32, (slots, rows), 0)
        expert = row // (batches * CAP)
        lower = (
            lax.broadcasted_iota(jnp.int32, (rows, rows), 0)
            < lax.broadcasted_iota(jnp.int32, (rows, rows), 1)
        ).astype(jnp.bfloat16)
        placed = []
        weighted = []
        for batch in range(batches):
            named = jnp.zeros((slots, rows), jnp.float32)
            weight = jnp.zeros((slots, rows), jnp.float32)
            for k in range(topk):
                hit = expert == ids_ref[batch, k : k + 1, :]
                named += jnp.where(hit, 1.0, 0.0)
                weight += jnp.where(hit, gate_ref[batch, k : k + 1, :], 0.0)
            rank = jnp.dot(named.astype(jnp.bfloat16), lower, preferred_element_type=jnp.float32)
            wanted = (row % (batches * CAP) - batch * CAP).astype(jnp.float32)
            here = jnp.where(rank == wanted, named, 0.0)
            placed.append(here)
            weighted.append(here * weight)
        slot_ref[...] = jnp.concatenate(placed, axis=1).astype(jnp.bfloat16)
        weight_ref[...] = jnp.concatenate(weighted, axis=1)

    width = quant_ref.shape[2]
    quant = quant_ref[...].reshape(tokens, width)
    scale = scale_ref[...].reshape(tokens, width // BLOCK)
    parts = []
    for block in range(width // BLOCK):
        values = quant[:, block * BLOCK : (block + 1) * BLOCK].astype(jnp.float32)
        parts.append((values * scale[:, block : block + 1]).astype(jnp.bfloat16))
    x = jnp.concatenate(parts, axis=1)
    send_ref[...] = jnp.dot(slot_ref[...], x, preferred_element_type=jnp.float32).astype(jnp.bfloat16)


def place_rows(quant, scales, ids, gates, experts):
    batches, rows, width = quant.shape
    tokens = batches * rows
    slots = experts * batches * CAP
    steps = 4
    step_width = width // steps
    step_blocks = step_width // BLOCK
    scales = scales.reshape(batches, rows, steps, step_blocks).transpose(2, 0, 1, 3)
    return pl.pallas_call(
        place_kernel,
        grid=(steps,),
        in_specs=[
            pl.BlockSpec((batches, rows, step_width), lambda i: (0, 0, i)),
            pl.BlockSpec((None, batches, rows, step_blocks), lambda i: (i, 0, 0, 0)),
            pl.BlockSpec(ids.shape, lambda i: (0, 0, 0)),
            pl.BlockSpec(gates.shape, lambda i: (0, 0, 0)),
        ],
        out_specs=[
            pl.BlockSpec((slots, step_width), lambda i: (0, i)),
            pl.BlockSpec((slots, tokens), lambda i: (0, 0)),
        ],
        out_shape=[
            jax.ShapeDtypeStruct((slots, width), jnp.bfloat16),
            jax.ShapeDtypeStruct((slots, tokens), jnp.float32),
        ],
        scratch_shapes=[pltpu.VMEM((slots, tokens), jnp.bfloat16)],
        compiler_params=pltpu.CompilerParams(vmem_limit_bytes=VMEM_LIMIT),
        cost_estimate=pl.CostEstimate(
            flops=2 * slots * tokens * width, bytes_accessed=2 * slots * width, transcendentals=0
        ),
    )(quant, scales, ids, gates)


ROW_TILE = 256


def expert_kernel(n_hidden, x_ref, gate_ref, up_ref, down_ref, y_ref, hidden_ref):
    step = pl.program_id(0)
    rows = x_ref.shape[0]
    tile = gate_ref.shape[1]

    @pl.when(step < n_hidden)
    def _():
        def body(i, carry):
            at = pl.ds(pl.multiple_of(i * ROW_TILE, ROW_TILE), ROW_TILE)
            x = x_ref[at, :]
            gate = jnp.dot(x, gate_ref[...], preferred_element_type=jnp.float32)
            upper = jnp.dot(x, up_ref[...], preferred_element_type=jnp.float32)
            hidden = gate / (1.0 + jnp.exp(-gate)) * upper
            hidden_ref[step, at, :] = hidden.astype(jnp.bfloat16)
            return carry

        lax.fori_loop(0, rows // ROW_TILE, body, 0)

    @pl.when(step >= n_hidden)
    def _():
        def body(i, carry):
            at = pl.ds(pl.multiple_of(i * ROW_TILE, ROW_TILE), ROW_TILE)
            total = jnp.dot(
                jnp.concatenate([hidden_ref[s, at, :] for s in range(n_hidden)], axis=1),
                down_ref[...],
                preferred_element_type=jnp.float32,
            )
            y_ref[at, :] = total.astype(jnp.bfloat16)
            return carry

        lax.fori_loop(0, rows // ROW_TILE, body, 0)


def expert_rows(x, gate_w, up_w, down_w):
    rows, width = x.shape
    hidden = gate_w.shape[1]
    hidden_tile = 256
    out_tile = 512
    n_hidden = hidden // hidden_tile
    n_out = width // out_tile
    first = lambda i: (0, jnp.minimum(i, n_hidden - 1))
    second = lambda i: (0, jnp.maximum(i - n_hidden, 0))
    return pl.pallas_call(
        functools.partial(expert_kernel, n_hidden),
        grid=(n_hidden + n_out,),
        in_specs=[
            pl.BlockSpec((rows, width), lambda i: (0, 0), pipeline_mode=pl.Buffered(1)),
            pl.BlockSpec((width, hidden_tile), first),
            pl.BlockSpec((width, hidden_tile), first),
            pl.BlockSpec((hidden, out_tile), second),
        ],
        out_specs=pl.BlockSpec((rows, out_tile), second),
        out_shape=jax.ShapeDtypeStruct((rows, width), jnp.bfloat16),
        scratch_shapes=[pltpu.VMEM((n_hidden, rows, hidden_tile), jnp.bfloat16)],
        compiler_params=pltpu.CompilerParams(vmem_limit_bytes=VMEM_LIMIT),
        cost_estimate=pl.CostEstimate(
            flops=6 * rows * width * hidden,
            bytes_accessed=6 * width * hidden + 4 * rows * width,
            transcendentals=rows * hidden,
        ),
    )(x, gate_w, up_w, down_w)


def combine_kernel(weight_ref, y_ref, out_ref):
    weight = weight_ref[...]
    high = weight.astype(jnp.bfloat16)
    low = (weight - high.astype(jnp.float32)).astype(jnp.bfloat16)
    both = jnp.concatenate([high, low], axis=1)
    tokens = weight.shape[1]
    y = y_ref[...]
    total = lax.dot_general(both, y, (((0,), (0,)), ((), ())), preferred_element_type=jnp.float32)
    out_ref[...] = (total[:tokens] + total[tokens:]).astype(jnp.bfloat16)


def combine(weights, y):
    slots, width = y.shape
    tokens = weights.shape[1]
    tile = 512
    return pl.pallas_call(
        combine_kernel,
        grid=(width // tile,),
        in_specs=[
            pl.BlockSpec((slots, tokens), lambda i: (0, 0)),
            pl.BlockSpec((slots, tile), lambda i: (0, i)),
        ],
        out_specs=pl.BlockSpec((tokens, tile), lambda i: (0, i)),
        out_shape=jax.ShapeDtypeStruct((tokens, width), jnp.bfloat16),
        compiler_params=pltpu.CompilerParams(vmem_limit_bytes=VMEM_LIMIT),
        cost_estimate=pl.CostEstimate(
            flops=4 * slots * tokens * width, bytes_accessed=2 * slots * width, transcendentals=0
        ),
    )(weights, y)


def shards(quant_rows, row_scales, expert_ids, gate_weights, w_gate, w_up, w_down):
    axes = ("group", "expert")
    experts = lax.axis_size("group") * lax.axis_size("expert")
    batches, rows, width = quant_rows.shape
    ids = expert_ids.transpose(0, 2, 1)
    gates = gate_weights.transpose(0, 2, 1)
    send, weights = place_rows(quant_rows, row_scales, ids, gates, experts)
    per_expert = batches * CAP
    got = lax.all_to_all(send.reshape(experts, per_expert, width), axes, 0, 0, tiled=True)
    answer = expert_rows(got.reshape(experts * per_expert, width), w_gate[0], w_up[0], w_down[0])
    back = lax.all_to_all(answer.reshape(experts, per_expert, width), axes, 0, 0, tiled=True)
    mixed = combine(weights, back.reshape(experts * per_expert, width))
    return mixed.reshape(batches, rows, width)


def solution(mesh):
    tokens = P(None, ("group", "expert"), None)
    weights = P(("group", "expert"), None, None)
    return jax.shard_map(
        shards,
        mesh=mesh,
        in_specs=(tokens, tokens, tokens, tokens, weights, weights, weights),
        out_specs=tokens,
        check_vma=False,
    )
```

```python
import functools

import jax
import jax.numpy as jnp
from jax import lax
from jax.experimental import pallas as pl
from jax.experimental.pallas import tpu as pltpu
from jax.sharding import PartitionSpec as P

BLOCK = 128
CAP = 4
ROW_TILE = 512
COLUMN_TILE = 512
HIDDEN_TILE = 256
MIB = 1024 * 1024
ANYWHERE = pl.BlockSpec(memory_space=pl.ANY)
IN_VMEM = pl.BlockSpec(memory_space=pltpu.VMEM)


def slot_matrix(ids, gates, slots, batches):
    topk, rows = ids[0].shape
    row = lax.broadcasted_iota(jnp.int32, (slots, rows), 0)
    expert = row // (batches * CAP)
    lower = (
        lax.broadcasted_iota(jnp.int32, (rows, rows), 0) < lax.broadcasted_iota(jnp.int32, (rows, rows), 1)
    ).astype(jnp.bfloat16)
    placed = []
    weighted = []
    for batch in range(batches):
        named = jnp.zeros((slots, rows), jnp.float32)
        weight = jnp.zeros((slots, rows), jnp.float32)
        for k in range(topk):
            hit = expert == ids[batch][k : k + 1, :]
            named += jnp.where(hit, 1.0, 0.0)
            if gates is not None:
                weight += jnp.where(hit, gates[batch][k : k + 1, :], 0.0)
        rank = jnp.dot(named.astype(jnp.bfloat16), lower, preferred_element_type=jnp.float32)
        wanted = (row % (batches * CAP) - batch * CAP).astype(jnp.float32)
        here = jnp.where(rank == wanted, named, 0.0)
        placed.append(here)
        weighted.append(here * weight)
    return jnp.concatenate(weighted if gates is not None else placed, axis=1)


def place_kernel(quant_hbm, scale_hbm, ids_hbm, send_ref, quant_ref, scale_ref, ids_ref, sems):
    batches, rows, width = quant_ref.shape
    slots = send_ref.shape[0]
    loads = [
        pltpu.make_async_copy(source, target, sems.at[i])
        for i, (source, target) in enumerate(
            ((ids_hbm, ids_ref), (scale_hbm, scale_ref), (quant_hbm, quant_ref))
        )
    ]
    for load in loads:
        load.start()
    loads[0].wait()
    placed = slot_matrix([ids_ref[b] for b in range(batches)], None, slots, batches).astype(jnp.bfloat16)
    loads[1].wait()
    scale = jnp.concatenate([scale_ref[:, b, :].T for b in range(batches)], axis=0)
    loads[2].wait()
    quant = quant_ref[...].reshape(batches * rows, width)
    for start in range(0, width, COLUMN_TILE):
        parts = []
        for block in range(start // BLOCK, (start + COLUMN_TILE) // BLOCK):
            values = quant[:, block * BLOCK : (block + 1) * BLOCK].astype(jnp.float32)
            parts.append((values * scale[:, block : block + 1]).astype(jnp.bfloat16))
        x = jnp.concatenate(parts, axis=1)
        send_ref[:, start : start + COLUMN_TILE] = jnp.dot(
            placed, x, preferred_element_type=jnp.float32
        ).astype(jnp.bfloat16)


def place_rows(quant, scales, ids, experts):
    batches, rows, width = quant.shape
    slots = experts * batches * CAP
    return pl.pallas_call(
        place_kernel,
        in_specs=[ANYWHERE, ANYWHERE, ANYWHERE],
        out_specs=IN_VMEM,
        out_shape=jax.ShapeDtypeStruct((slots, width), jnp.bfloat16),
        scratch_shapes=[
            pltpu.VMEM(quant.shape, quant.dtype),
            pltpu.VMEM(scales.shape, scales.dtype),
            pltpu.VMEM(ids.shape, ids.dtype),
            pltpu.SemaphoreType.DMA((3,)),
        ],
        compiler_params=pltpu.CompilerParams(vmem_limit_bytes=10 * MIB),
        cost_estimate=pl.CostEstimate(
            flops=2 * slots * batches * rows * width, bytes_accessed=2 * slots * width, transcendentals=0
        ),
    )(quant, scales, ids)


def expert_kernel(x_ref, gate_ref, up_ref, down_ref, ids_ref, gates_ref, y_ref, weight_ref, hidden_ref):
    rows, width = x_ref.shape
    batches = ids_ref.shape[0]
    tokens = weight_ref.shape[0] // 2
    weight = slot_matrix(
        [ids_ref[b] for b in range(batches)], [gates_ref[b] for b in range(batches)], weight_ref.shape[1], batches
    ).T
    high = weight.astype(jnp.bfloat16)
    weight_ref[0:tokens, :] = high
    weight_ref[tokens:, :] = (weight - high.astype(jnp.float32)).astype(jnp.bfloat16)
    hidden = hidden_ref.shape[1]
    for r in range(0, rows, ROW_TILE):
        at = slice(r, r + ROW_TILE)
        for c in range(0, hidden, HIDDEN_TILE):
            cols = slice(c, c + HIDDEN_TILE)
            gate = jnp.dot(x_ref[at, :], gate_ref[:, cols], preferred_element_type=jnp.float32)
            upper = jnp.dot(x_ref[at, :], up_ref[:, cols], preferred_element_type=jnp.float32)
            half = 0.5 * gate
            hidden_ref[at, cols] = (half * (1.0 + jnp.tanh(half)) * upper).astype(jnp.bfloat16)
    for r in range(0, rows, ROW_TILE):
        at = slice(r, r + ROW_TILE)
        for c in range(0, width, COLUMN_TILE):
            cols = slice(c, c + COLUMN_TILE)
            y_ref[at, cols] = jnp.dot(
                hidden_ref[at, :], down_ref[:, cols], preferred_element_type=jnp.float32
            ).astype(jnp.bfloat16)


def expert_rows(x, gate_w, up_w, down_w, ids, gates):
    rows, width = x.shape
    hidden = gate_w.shape[1]
    batches, _, tokens = ids.shape
    return pl.pallas_call(
        expert_kernel,
        in_specs=[IN_VMEM] * 6,
        out_specs=[IN_VMEM] * 2,
        out_shape=[
            jax.ShapeDtypeStruct((rows, width), jnp.bfloat16),
            jax.ShapeDtypeStruct((2 * batches * tokens, rows), jnp.bfloat16),
        ],
        scratch_shapes=[pltpu.VMEM((rows, hidden), jnp.bfloat16)],
        compiler_params=pltpu.CompilerParams(vmem_limit_bytes=10 * MIB),
        cost_estimate=pl.CostEstimate(
            flops=6 * rows * width * hidden,
            bytes_accessed=6 * width * hidden + 4 * rows * width,
            transcendentals=rows * hidden,
        ),
    )(x, gate_w, up_w, down_w, ids, gates)


def combine_kernel(weight_ref, y_ref, out_ref):
    tokens = out_ref.shape[0]
    for c in range(0, y_ref.shape[1], COLUMN_TILE):
        cols = slice(c, c + COLUMN_TILE)
        total = jnp.dot(weight_ref[...], y_ref[:, cols], preferred_element_type=jnp.float32)
        out_ref[:, cols] = (total[:tokens] + total[tokens:]).astype(jnp.bfloat16)


def combine(weights, y):
    slots, width = y.shape
    tokens = weights.shape[0] // 2
    return pl.pallas_call(
        combine_kernel,
        in_specs=[IN_VMEM, IN_VMEM],
        out_specs=IN_VMEM,
        out_shape=jax.ShapeDtypeStruct((tokens, width), jnp.bfloat16),
        compiler_params=pltpu.CompilerParams(vmem_limit_bytes=10 * MIB),
        cost_estimate=pl.CostEstimate(
            flops=4 * slots * tokens * width, bytes_accessed=2 * slots * width, transcendentals=0
        ),
    )(weights, y)


def shards(quant_rows, row_scales, expert_ids, gate_weights, w_gate, w_up, w_down):
    axes = ("group", "expert")
    experts = lax.axis_size("group") * lax.axis_size("expert")
    batches, rows, width = quant_rows.shape
    ids = expert_ids.transpose(0, 2, 1)
    gates = gate_weights.transpose(0, 2, 1)
    send = place_rows(quant_rows, row_scales.transpose(2, 0, 1), ids, experts)
    per_expert = batches * CAP
    got = lax.all_to_all(send.reshape(experts, per_expert, width), axes, 0, 0, tiled=True)
    answer, weights = expert_rows(
        got.reshape(experts * per_expert, width), w_gate[0], w_up[0], w_down[0], ids, gates
    )
    back = lax.all_to_all(answer.reshape(experts, per_expert, width), axes, 0, 0, tiled=True)
    mixed = combine(weights, back.reshape(experts * per_expert, width))
    return mixed.reshape(batches, rows, width)


def solution(mesh):
    tokens = P(None, ("group", "expert"), None)
    weights = P(("group", "expert"), None, None)
    return jax.shard_map(
        shards,
        mesh=mesh,
        in_specs=(tokens, tokens, tokens, tokens, weights, weights, weights),
        out_specs=tokens,
        check_vma=False,
    )
```

```python
import functools

import jax
import jax.numpy as jnp
from jax import lax
from jax.experimental import pallas as pl
from jax.experimental.pallas import tpu as pltpu
from jax.sharding import PartitionSpec as P

BLOCK = 128
CAP = 4
ROW_TILE = 512
COLUMN_TILE = 512
HIDDEN_TILE = 256
WEIGHT_TILE = 128
MIB = 1024 * 1024
IN_VMEM = pl.BlockSpec(memory_space=pltpu.VMEM)


def slot_matrix(ids, gates, first, experts, batches):
    topk, tokens = ids.shape
    rows = tokens // batches
    per_expert = batches * CAP
    expert = lax.broadcasted_iota(jnp.int32, (experts, tokens), 0) + first
    named = jnp.zeros((experts, tokens), jnp.float32)
    weight = jnp.zeros((experts, tokens), jnp.float32)
    for k in range(topk):
        hit = expert == ids[k : k + 1, :]
        named += jnp.where(hit, 1.0, 0.0)
        if gates is not None:
            weight += jnp.where(hit, gates[k : k + 1, :], 0.0)
    ahead = lax.broadcasted_iota(jnp.int32, (tokens, tokens), 0)
    token = lax.broadcasted_iota(jnp.int32, (tokens, tokens), 1)
    lower = jnp.logical_and(ahead < token, ahead // rows == token // rows)
    rank = jnp.dot(
        named.astype(jnp.bfloat16),
        jnp.where(lower, 1.0, 0.0).astype(jnp.bfloat16),
        preferred_element_type=jnp.float32,
    )
    slot = lax.broadcasted_iota(jnp.int32, (1, per_expert, tokens), 1)
    slot -= CAP * (lax.broadcasted_iota(jnp.int32, (1, per_expert, tokens), 2) // rows)
    value = named if gates is None else weight
    shape = (experts, per_expert, tokens)
    here = jnp.broadcast_to(rank[:, None, :], shape) == slot.astype(jnp.float32)
    live = jnp.logical_and(here, jnp.broadcast_to(named[:, None, :], shape) > 0.0)
    placed = jnp.where(live, jnp.broadcast_to(value[:, None, :], shape), 0.0)
    return placed.reshape(experts * per_expert, tokens)


def place_kernel(quant_ref, scale_ref, ids_ref, send_ref):
    batches, rows, width = quant_ref.shape
    slots = send_ref.shape[0]
    ids = jnp.concatenate([ids_ref[b] for b in range(batches)], axis=1)
    placed = slot_matrix(ids, None, 0, slots // (batches * CAP), batches).astype(jnp.bfloat16)
    scale = jnp.concatenate([scale_ref[:, b, :].T for b in range(batches)], axis=0)
    quant = quant_ref[...].reshape(batches * rows, width)
    for start in range(0, width, COLUMN_TILE):
        parts = []
        for block in range(start // BLOCK, (start + COLUMN_TILE) // BLOCK):
            values = quant[:, block * BLOCK : (block + 1) * BLOCK].astype(jnp.float32)
            parts.append((values * scale[:, block : block + 1]).astype(jnp.bfloat16))
        x = jnp.concatenate(parts, axis=1)
        send_ref[:, start : start + COLUMN_TILE] = jnp.dot(
            placed, x, preferred_element_type=jnp.float32
        ).astype(jnp.bfloat16)


def place_rows(quant, scales, ids, experts):
    batches, rows, width = quant.shape
    slots = experts * batches * CAP
    return pl.pallas_call(
        place_kernel,
        in_specs=[IN_VMEM, IN_VMEM, IN_VMEM],
        out_specs=IN_VMEM,
        out_shape=jax.ShapeDtypeStruct((slots, width), jnp.bfloat16),
        compiler_params=pltpu.CompilerParams(vmem_limit_bytes=10 * MIB),
        cost_estimate=pl.CostEstimate(
            flops=2 * slots * batches * rows * width, bytes_accessed=2 * slots * width, transcendentals=0
        ),
    )(quant, scales, ids)


def expert_kernel(x_ref, gate_ref, up_ref, down_ref, ids_ref, gates_ref, y_ref, weight_ref, hidden_ref):
    rows, width = x_ref.shape
    batches = ids_ref.shape[0]
    tokens = weight_ref.shape[0] // 2
    ids = jnp.concatenate([ids_ref[b] for b in range(batches)], axis=1)
    gates = jnp.concatenate([gates_ref[b] for b in range(batches)], axis=1)
    per_expert = batches * CAP

    def weigh(first):
        weight = slot_matrix(ids, gates, first // per_expert, WEIGHT_TILE // per_expert, batches).T
        high = weight.astype(jnp.bfloat16)
        at = slice(first, first + WEIGHT_TILE)
        weight_ref[0:tokens, at] = high
        weight_ref[tokens:, at] = (weight - high.astype(jnp.float32)).astype(jnp.bfloat16)

    pieces = list(range(0, rows, WEIGHT_TILE))
    hidden = hidden_ref.shape[1]
    for r in range(0, rows, ROW_TILE):
        at = slice(r, r + ROW_TILE)
        for c in range(0, hidden, HIDDEN_TILE):
            cols = slice(c, c + HIDDEN_TILE)
            gate = jnp.dot(x_ref[at, :], gate_ref[:, cols], preferred_element_type=jnp.float32)
            upper = jnp.dot(x_ref[at, :], up_ref[:, cols], preferred_element_type=jnp.float32)
            half = 0.5 * gate
            hidden_ref[at, cols] = (half * (1.0 + jnp.tanh(half)) * upper).astype(jnp.bfloat16)
    for r in range(0, rows, ROW_TILE):
        at = slice(r, r + ROW_TILE)
        for c in range(0, width, COLUMN_TILE):
            cols = slice(c, c + COLUMN_TILE)
            y_ref[at, cols] = jnp.dot(
                hidden_ref[at, :], down_ref[:, cols], preferred_element_type=jnp.float32
            ).astype(jnp.bfloat16)
            if pieces:
                weigh(pieces.pop(0))


def expert_rows(x, gate_w, up_w, down_w, ids, gates):
    rows, width = x.shape
    hidden = gate_w.shape[1]
    batches, _, tokens = ids.shape
    return pl.pallas_call(
        expert_kernel,
        in_specs=[IN_VMEM] * 6,
        out_specs=[IN_VMEM] * 2,
        out_shape=[
            jax.ShapeDtypeStruct((rows, width), jnp.bfloat16),
            jax.ShapeDtypeStruct((2 * batches * tokens, rows), jnp.bfloat16),
        ],
        scratch_shapes=[pltpu.VMEM((rows, hidden), jnp.bfloat16)],
        compiler_params=pltpu.CompilerParams(vmem_limit_bytes=10 * MIB),
        cost_estimate=pl.CostEstimate(
            flops=6 * rows * width * hidden,
            bytes_accessed=6 * width * hidden + 4 * rows * width,
            transcendentals=rows * hidden,
        ),
    )(x, gate_w, up_w, down_w, ids, gates)


def combine_kernel(weight_ref, y_ref, out_ref):
    tokens = out_ref.shape[0]
    for c in range(0, y_ref.shape[1], COLUMN_TILE):
        cols = slice(c, c + COLUMN_TILE)
        total = jnp.dot(weight_ref[...], y_ref[:, cols], preferred_element_type=jnp.float32)
        out_ref[:, cols] = (total[:tokens] + total[tokens:]).astype(jnp.bfloat16)


def combine(weights, y):
    slots, width = y.shape
    tokens = weights.shape[0] // 2
    return pl.pallas_call(
        combine_kernel,
        in_specs=[IN_VMEM, IN_VMEM],
        out_specs=IN_VMEM,
        out_shape=jax.ShapeDtypeStruct((tokens, width), jnp.bfloat16),
        compiler_params=pltpu.CompilerParams(vmem_limit_bytes=10 * MIB),
        cost_estimate=pl.CostEstimate(
            flops=4 * slots * tokens * width, bytes_accessed=2 * slots * width, transcendentals=0
        ),
    )(weights, y)


def shards(quant_rows, row_scales, expert_ids, gate_weights, w_gate, w_up, w_down):
    axes = ("group", "expert")
    experts = lax.axis_size("group") * lax.axis_size("expert")
    batches, rows, width = quant_rows.shape
    ids = expert_ids.transpose(0, 2, 1)
    gates = gate_weights.transpose(0, 2, 1)
    send = place_rows(quant_rows, row_scales.transpose(2, 0, 1), ids, experts)
    per_expert = batches * CAP
    got = lax.all_to_all(send.reshape(experts, per_expert, width), axes, 0, 0, tiled=True)
    answer, weights = expert_rows(
        got.reshape(experts * per_expert, width), w_gate[0], w_up[0], w_down[0], ids, gates
    )
    back = lax.all_to_all(answer.reshape(experts, per_expert, width), axes, 0, 0, tiled=True)
    mixed = combine(weights, back.reshape(experts * per_expert, width))
    return mixed.reshape(batches, rows, width)


def solution(mesh):
    tokens = P(None, ("group", "expert"), None)
    weights = P(("group", "expert"), None, None)
    return jax.shard_map(
        shards,
        mesh=mesh,
        in_specs=(tokens, tokens, tokens, tokens, weights, weights, weights),
        out_specs=tokens,
        check_vma=False,
    )
```

```python
import functools

import jax
import jax.numpy as jnp
from jax import lax
from jax.experimental import pallas as pl
from jax.experimental.pallas import tpu as pltpu
from jax.sharding import PartitionSpec as P

BLOCK = 128
CAP = 4
ROW_TILE = 512
COLUMN_TILE = 512
HIDDEN_TILE = 256
WEIGHT_TILE = 128
MIB = 1024 * 1024
ROUTE_VMEM = 53 * MIB
IN_VMEM = pl.BlockSpec(memory_space=pltpu.VMEM)


def slot_matrix(ids, gates, first, experts, batches):
    topk, tokens = ids.shape
    rows = tokens // batches
    per_expert = batches * CAP
    expert = lax.broadcasted_iota(jnp.int32, (experts, tokens), 0) + first
    named = jnp.zeros((experts, tokens), jnp.float32)
    weight = jnp.zeros((experts, tokens), jnp.float32)
    for k in range(topk):
        hit = expert == ids[k : k + 1, :]
        named += jnp.where(hit, 1.0, 0.0)
        if gates is not None:
            weight += jnp.where(hit, gates[k : k + 1, :], 0.0)
    ahead = lax.broadcasted_iota(jnp.int32, (tokens, tokens), 0)
    token = lax.broadcasted_iota(jnp.int32, (tokens, tokens), 1)
    lower = jnp.logical_and(ahead < token, ahead // rows == token // rows)
    rank = jnp.dot(
        named.astype(jnp.bfloat16),
        jnp.where(lower, 1.0, 0.0).astype(jnp.bfloat16),
        preferred_element_type=jnp.float32,
    )
    slot = lax.broadcasted_iota(jnp.int32, (1, per_expert, tokens), 1)
    slot -= CAP * (lax.broadcasted_iota(jnp.int32, (1, per_expert, tokens), 2) // rows)
    value = named if gates is None else weight
    shape = (experts, per_expert, tokens)
    here = jnp.broadcast_to(rank[:, None, :], shape) == slot.astype(jnp.float32)
    live = jnp.logical_and(here, jnp.broadcast_to(named[:, None, :], shape) > 0.0)
    placed = jnp.where(live, jnp.broadcast_to(value[:, None, :], shape), 0.0)
    return placed.reshape(experts * per_expert, tokens)


def route_kernel(quant_hbm, scale_hbm, ids_hbm, x_ref, placed_ref, quant_ref, scale_ref, ids_ref, sems):
    batches, rows, width = quant_ref.shape
    loads = [
        pltpu.make_async_copy(source, target, sems.at[i])
        for i, (source, target) in enumerate(
            ((ids_hbm, ids_ref), (scale_hbm, scale_ref), (quant_hbm, quant_ref))
        )
    ]
    for load in loads:
        load.start()
    loads[0].wait()
    ids = jnp.concatenate([ids_ref[b] for b in range(batches)], axis=1)
    experts = placed_ref.shape[0] // (batches * CAP)
    placed_ref[...] = slot_matrix(ids, None, 0, experts, batches).astype(jnp.bfloat16)
    loads[1].wait()
    scale = jnp.concatenate([scale_ref[:, b, :].T for b in range(batches)], axis=0)
    loads[2].wait()
    quant = quant_ref[...].reshape(batches * rows, width)
    for block in range(width // BLOCK):
        cols = slice(block * BLOCK, (block + 1) * BLOCK)
        x_ref[:, cols] = (quant[:, cols].astype(jnp.float32) * scale[:, block : block + 1]).astype(jnp.bfloat16)


def route(quant, scales, ids, experts):
    batches, rows, width = quant.shape
    slots = experts * batches * CAP
    anywhere = pl.BlockSpec(memory_space=pl.ANY)
    return pl.pallas_call(
        route_kernel,
        in_specs=[anywhere] * 3,
        out_specs=[IN_VMEM] * 2,
        out_shape=[
            jax.ShapeDtypeStruct((batches * rows, width), jnp.bfloat16),
            jax.ShapeDtypeStruct((slots, batches * rows), jnp.bfloat16),
        ],
        scratch_shapes=[
            pltpu.VMEM(quant.shape, quant.dtype),
            pltpu.VMEM(scales.shape, scales.dtype),
            pltpu.VMEM(ids.shape, ids.dtype),
            pltpu.SemaphoreType.DMA((3,)),
        ],
        compiler_params=pltpu.CompilerParams(vmem_limit_bytes=ROUTE_VMEM),
        cost_estimate=pl.CostEstimate(
            flops=8 * slots * batches * rows, bytes_accessed=4 * batches * rows * width, transcendentals=0
        ),
    )(quant, scales, ids)


def place_kernel(placed_ref, x_ref, send_ref):
    for start in range(0, x_ref.shape[1], COLUMN_TILE):
        cols = slice(start, start + COLUMN_TILE)
        send_ref[:, cols] = jnp.dot(
            placed_ref[...], x_ref[:, cols], preferred_element_type=jnp.float32
        ).astype(jnp.bfloat16)


def place_rows(placed, x):
    tokens, width = x.shape
    slots = placed.shape[0]
    return pl.pallas_call(
        place_kernel,
        in_specs=[IN_VMEM] * 2,
        out_specs=IN_VMEM,
        out_shape=jax.ShapeDtypeStruct((slots, width), jnp.bfloat16),
        compiler_params=pltpu.CompilerParams(vmem_limit_bytes=10 * MIB),
        cost_estimate=pl.CostEstimate(
            flops=2 * slots * tokens * width, bytes_accessed=2 * slots * width, transcendentals=0
        ),
    )(placed, x)


def expert_kernel(x_ref, gate_ref, up_ref, down_ref, ids_ref, gates_ref, y_ref, weight_ref, hidden_ref):
    rows, width = x_ref.shape
    batches = ids_ref.shape[0]
    tokens = weight_ref.shape[0] // 2
    ids = jnp.concatenate([ids_ref[b] for b in range(batches)], axis=1)
    gates = jnp.concatenate([gates_ref[b] for b in range(batches)], axis=1)
    per_expert = batches * CAP

    def weigh(first):
        weight = slot_matrix(ids, gates, first // per_expert, WEIGHT_TILE // per_expert, batches).T
        high = weight.astype(jnp.bfloat16)
        at = slice(first, first + WEIGHT_TILE)
        weight_ref[0:tokens, at] = high
        weight_ref[tokens:, at] = (weight - high.astype(jnp.float32)).astype(jnp.bfloat16)

    pieces = list(range(0, rows, WEIGHT_TILE))
    hidden = hidden_ref.shape[1]
    for r in range(0, rows, ROW_TILE):
        at = slice(r, r + ROW_TILE)
        for c in range(0, hidden, HIDDEN_TILE):
            cols = slice(c, c + HIDDEN_TILE)
            gate = jnp.dot(x_ref[at, :], gate_ref[:, cols], preferred_element_type=jnp.float32)
            upper = jnp.dot(x_ref[at, :], up_ref[:, cols], preferred_element_type=jnp.float32)
            half = 0.5 * gate
            hidden_ref[at, cols] = (half * (1.0 + jnp.tanh(half)) * upper).astype(jnp.bfloat16)
    for r in range(0, rows, ROW_TILE):
        at = slice(r, r + ROW_TILE)
        for c in range(0, width, COLUMN_TILE):
            cols = slice(c, c + COLUMN_TILE)
            y_ref[at, cols] = jnp.dot(
                hidden_ref[at, :], down_ref[:, cols], preferred_element_type=jnp.float32
            ).astype(jnp.bfloat16)
            if pieces:
                weigh(pieces.pop(0))


def expert_rows(x, gate_w, up_w, down_w, ids, gates):
    rows, width = x.shape
    hidden = gate_w.shape[1]
    batches, _, tokens = ids.shape
    return pl.pallas_call(
        expert_kernel,
        in_specs=[IN_VMEM] * 6,
        out_specs=[IN_VMEM] * 2,
        out_shape=[
            jax.ShapeDtypeStruct((rows, width), jnp.bfloat16),
            jax.ShapeDtypeStruct((2 * batches * tokens, rows), jnp.bfloat16),
        ],
        scratch_shapes=[pltpu.VMEM((rows, hidden), jnp.bfloat16)],
        compiler_params=pltpu.CompilerParams(vmem_limit_bytes=10 * MIB),
        cost_estimate=pl.CostEstimate(
            flops=6 * rows * width * hidden,
            bytes_accessed=6 * width * hidden + 4 * rows * width,
            transcendentals=rows * hidden,
        ),
    )(x, gate_w, up_w, down_w, ids, gates)


def combine_kernel(weight_ref, y_ref, out_ref):
    tokens = out_ref.shape[0]
    for c in range(0, y_ref.shape[1], COLUMN_TILE):
        cols = slice(c, c + COLUMN_TILE)
        total = jnp.dot(weight_ref[...], y_ref[:, cols], preferred_element_type=jnp.float32)
        out_ref[:, cols] = (total[:tokens] + total[tokens:]).astype(jnp.bfloat16)


def combine(weights, y):
    slots, width = y.shape
    tokens = weights.shape[0] // 2
    return pl.pallas_call(
        combine_kernel,
        in_specs=[IN_VMEM, IN_VMEM],
        out_specs=IN_VMEM,
        out_shape=jax.ShapeDtypeStruct((tokens, width), jnp.bfloat16),
        compiler_params=pltpu.CompilerParams(vmem_limit_bytes=10 * MIB),
        cost_estimate=pl.CostEstimate(
            flops=4 * slots * tokens * width, bytes_accessed=2 * slots * width, transcendentals=0
        ),
    )(weights, y)


def shards(quant_rows, row_scales, expert_ids, gate_weights, w_gate, w_up, w_down):
    axes = ("group", "expert")
    experts = lax.axis_size("group") * lax.axis_size("expert")
    batches, rows, width = quant_rows.shape
    ids = expert_ids.transpose(0, 2, 1)
    gates = gate_weights.transpose(0, 2, 1)
    x, placed = route(quant_rows, row_scales.transpose(2, 0, 1), ids, experts)
    send = place_rows(placed, x)
    per_expert = batches * CAP
    got = lax.all_to_all(send.reshape(experts, per_expert, width), axes, 0, 0, tiled=True)
    answer, weights = expert_rows(
        got.reshape(experts * per_expert, width), w_gate[0], w_up[0], w_down[0], ids, gates
    )
    back = lax.all_to_all(answer.reshape(experts, per_expert, width), axes, 0, 0, tiled=True)
    mixed = combine(weights, back.reshape(experts * per_expert, width))
    return mixed.reshape(batches, rows, width)


def solution(mesh):
    tokens = P(None, ("group", "expert"), None)
    weights = P(("group", "expert"), None, None)
    return jax.shard_map(
        shards,
        mesh=mesh,
        in_specs=(tokens, tokens, tokens, tokens, weights, weights, weights),
        out_specs=tokens,
        check_vma=False,
    )
```

```python
import functools

import jax
import jax.numpy as jnp
from jax import lax
from jax.experimental import pallas as pl
from jax.experimental.pallas import tpu as pltpu
from jax.sharding import PartitionSpec as P

BLOCK = 128
CAP = 4
ROW_TILE = 512
COLUMN_TILE = 512
HIDDEN_TILE = 256
WEIGHT_TILE = 128
MIB = 1024 * 1024
ROUTE_VMEM = 53 * MIB
IN_VMEM = pl.BlockSpec(memory_space=pltpu.VMEM)


def slot_matrix(ids, gates, first, experts, batches):
    topk, tokens = ids.shape
    rows = tokens // batches
    per_expert = batches * CAP
    expert = lax.broadcasted_iota(jnp.int32, (experts, tokens), 0) + first
    named = jnp.zeros((experts, tokens), jnp.float32)
    weight = jnp.zeros((experts, tokens), jnp.float32)
    for k in range(topk):
        hit = expert == ids[k : k + 1, :]
        named += jnp.where(hit, 1.0, 0.0)
        if gates is not None:
            weight += jnp.where(hit, gates[k : k + 1, :], 0.0)
    ahead = lax.broadcasted_iota(jnp.int32, (tokens, tokens), 0)
    token = lax.broadcasted_iota(jnp.int32, (tokens, tokens), 1)
    lower = jnp.logical_and(ahead < token, ahead // rows == token // rows)
    rank = jnp.dot(
        named.astype(jnp.bfloat16),
        jnp.where(lower, 1.0, 0.0).astype(jnp.bfloat16),
        preferred_element_type=jnp.float32,
    )
    slot = lax.broadcasted_iota(jnp.int32, (1, per_expert, tokens), 1)
    slot -= CAP * (lax.broadcasted_iota(jnp.int32, (1, per_expert, tokens), 2) // rows)
    value = named if gates is None else weight
    shape = (experts, per_expert, tokens)
    here = jnp.broadcast_to(rank[:, None, :], shape) == slot.astype(jnp.float32)
    live = jnp.logical_and(here, jnp.broadcast_to(named[:, None, :], shape) > 0.0)
    placed = jnp.where(live, jnp.broadcast_to(value[:, None, :], shape), 0.0)
    return placed.reshape(experts * per_expert, tokens)


def route_kernel(quant_hbm, scale_hbm, ids_hbm, x_ref, placed_ref, quant_ref, scale_ref, ids_ref, sems):
    batches, rows, width = quant_ref.shape
    loads = [
        pltpu.make_async_copy(source, target, sems.at[i])
        for i, (source, target) in enumerate(
            ((ids_hbm, ids_ref), (scale_hbm, scale_ref), (quant_hbm, quant_ref))
        )
    ]
    for load in loads:
        load.start()
    loads[0].wait()
    ids = jnp.concatenate([ids_ref[b] for b in range(batches)], axis=1)
    experts = placed_ref.shape[0] // (batches * CAP)
    placed_ref[...] = slot_matrix(ids, None, 0, experts, batches).astype(jnp.bfloat16)
    loads[1].wait()
    scale = jnp.concatenate([scale_ref[:, b, :].T for b in range(batches)], axis=0)
    loads[2].wait()
    quant = quant_ref[...].reshape(batches * rows, width)
    for block in range(width // BLOCK):
        cols = slice(block * BLOCK, (block + 1) * BLOCK)
        x_ref[:, cols] = (quant[:, cols].astype(jnp.float32) * scale[:, block : block + 1]).astype(jnp.bfloat16)


def route(quant, scales, ids, experts):
    batches, rows, width = quant.shape
    slots = experts * batches * CAP
    anywhere = pl.BlockSpec(memory_space=pl.ANY)
    return pl.pallas_call(
        route_kernel,
        in_specs=[anywhere] * 3,
        out_specs=[IN_VMEM] * 2,
        out_shape=[
            jax.ShapeDtypeStruct((batches * rows, width), jnp.bfloat16),
            jax.ShapeDtypeStruct((slots, batches * rows), jnp.bfloat16),
        ],
        scratch_shapes=[
            pltpu.VMEM(quant.shape, quant.dtype),
            pltpu.VMEM(scales.shape, scales.dtype),
            pltpu.VMEM(ids.shape, ids.dtype),
            pltpu.SemaphoreType.DMA((3,)),
        ],
        compiler_params=pltpu.CompilerParams(vmem_limit_bytes=ROUTE_VMEM),
        cost_estimate=pl.CostEstimate(
            flops=8 * slots * batches * rows, bytes_accessed=4 * batches * rows * width, transcendentals=0
        ),
    )(quant, scales, ids)


def place_kernel(placed_ref, x_ref, send_ref):
    for start in range(0, x_ref.shape[1], COLUMN_TILE):
        cols = slice(start, start + COLUMN_TILE)
        send_ref[:, cols] = jnp.dot(
            placed_ref[...], x_ref[:, cols], preferred_element_type=jnp.float32
        ).astype(jnp.bfloat16)


def place_rows(placed, x):
    tokens, width = x.shape
    slots = placed.shape[0]
    return pl.pallas_call(
        place_kernel,
        in_specs=[IN_VMEM] * 2,
        out_specs=IN_VMEM,
        out_shape=jax.ShapeDtypeStruct((slots, width), jnp.bfloat16),
        compiler_params=pltpu.CompilerParams(vmem_limit_bytes=10 * MIB),
        cost_estimate=pl.CostEstimate(
            flops=2 * slots * tokens * width, bytes_accessed=2 * slots * width, transcendentals=0
        ),
    )(placed, x)


def expert_kernel(x_ref, gate_ref, up_ref, down_ref, ids_ref, gates_ref, y_ref, weight_ref, hidden_ref):
    rows, width = x_ref.shape
    batches = ids_ref.shape[0]
    tokens = weight_ref.shape[0] // 2
    ids = jnp.concatenate([ids_ref[b] for b in range(batches)], axis=1)
    gates = jnp.concatenate([gates_ref[b] for b in range(batches)], axis=1)
    per_expert = batches * CAP

    def weigh(first):
        weight = slot_matrix(ids, gates, first // per_expert, WEIGHT_TILE // per_expert, batches).T
        high = weight.astype(jnp.bfloat16)
        at = slice(first, first + WEIGHT_TILE)
        weight_ref[0:tokens, at] = high
        weight_ref[tokens:, at] = (weight - high.astype(jnp.float32)).astype(jnp.bfloat16)

    pieces = list(range(0, rows, WEIGHT_TILE))
    hidden = hidden_ref.shape[1]
    for r in range(0, rows, ROW_TILE):
        at = slice(r, r + ROW_TILE)
        for c in range(0, hidden, HIDDEN_TILE):
            cols = slice(c, c + HIDDEN_TILE)
            gate = jnp.dot(x_ref[at, :], gate_ref[:, cols], preferred_element_type=jnp.float32)
            upper = jnp.dot(x_ref[at, :], up_ref[:, cols], preferred_element_type=jnp.float32)
            half = 0.5 * gate
            hidden_ref[at, cols] = (half * (1.0 + jnp.tanh(half)) * upper).astype(jnp.bfloat16)
    for r in range(0, rows, ROW_TILE):
        at = slice(r, r + ROW_TILE)
        for c in range(0, width, COLUMN_TILE):
            cols = slice(c, c + COLUMN_TILE)
            y_ref[at, cols] = jnp.dot(
                hidden_ref[at, :], down_ref[:, cols], preferred_element_type=jnp.float32
            ).astype(jnp.bfloat16)
            if pieces:
                weigh(pieces.pop(0))


def expert_rows(x, gate_w, up_w, down_w, ids, gates):
    rows, width = x.shape
    hidden = gate_w.shape[1]
    batches, _, tokens = ids.shape
    return pl.pallas_call(
        expert_kernel,
        in_specs=[IN_VMEM] * 6,
        out_specs=[IN_VMEM] * 2,
        out_shape=[
            jax.ShapeDtypeStruct((rows, width), jnp.bfloat16),
            jax.ShapeDtypeStruct((2 * batches * tokens, rows), jnp.bfloat16),
        ],
        scratch_shapes=[pltpu.VMEM((rows, hidden), jnp.bfloat16)],
        compiler_params=pltpu.CompilerParams(vmem_limit_bytes=10 * MIB),
        cost_estimate=pl.CostEstimate(
            flops=6 * rows * width * hidden,
            bytes_accessed=6 * width * hidden + 4 * rows * width,
            transcendentals=rows * hidden,
        ),
    )(x, gate_w, up_w, down_w, ids, gates)


def combine_kernel(weight_ref, y_ref, out_hbm, out_ref, sems):
    tokens, width = out_ref.shape
    stores = []
    for c in range(0, width, COLUMN_TILE):
        cols = slice(c, c + COLUMN_TILE)
        total = jnp.dot(weight_ref[...], y_ref[:, cols], preferred_element_type=jnp.float32)
        out_ref[:, cols] = (total[:tokens] + total[tokens:]).astype(jnp.bfloat16)
        at = pl.ds(c, COLUMN_TILE)
        stores.append(pltpu.make_async_copy(out_ref.at[:, at], out_hbm.at[:, at], sems.at[c // COLUMN_TILE]))
        stores[-1].start()
    for store in stores:
        store.wait()


def combine(weights, y):
    slots, width = y.shape
    tokens = weights.shape[0] // 2
    return pl.pallas_call(
        combine_kernel,
        in_specs=[IN_VMEM, IN_VMEM],
        out_specs=pl.BlockSpec(memory_space=pl.ANY),
        out_shape=jax.ShapeDtypeStruct((tokens, width), jnp.bfloat16),
        scratch_shapes=[
            pltpu.VMEM((tokens, width), jnp.bfloat16),
            pltpu.SemaphoreType.DMA((width // COLUMN_TILE,)),
        ],
        compiler_params=pltpu.CompilerParams(vmem_limit_bytes=10 * MIB),
        cost_estimate=pl.CostEstimate(
            flops=4 * slots * tokens * width, bytes_accessed=2 * slots * width, transcendentals=0
        ),
    )(weights, y)


def shards(quant_rows, row_scales, expert_ids, gate_weights, w_gate, w_up, w_down):
    axes = ("group", "expert")
    experts = lax.axis_size("group") * lax.axis_size("expert")
    batches, rows, width = quant_rows.shape
    ids = expert_ids.transpose(0, 2, 1)
    gates = gate_weights.transpose(0, 2, 1)
    x, placed = route(quant_rows, row_scales.transpose(2, 0, 1), ids, experts)
    send = place_rows(placed, x)
    per_expert = batches * CAP
    got = lax.all_to_all(send.reshape(experts, per_expert, width), axes, 0, 0, tiled=True)
    answer, weights = expert_rows(
        got.reshape(experts * per_expert, width), w_gate[0], w_up[0], w_down[0], ids, gates
    )
    back = lax.all_to_all(answer.reshape(experts, per_expert, width), axes, 0, 0, tiled=True)
    mixed = combine(weights, back.reshape(experts * per_expert, width))
    return mixed.reshape(batches, rows, width)


def solution(mesh):
    tokens = P(None, ("group", "expert"), None)
    weights = P(("group", "expert"), None, None)
    return jax.shard_map(
        shards,
        mesh=mesh,
        in_specs=(tokens, tokens, tokens, tokens, weights, weights, weights),
        out_specs=tokens,
        check_vma=False,
    )
```
